32 devices in a mesh: rep: 2 (over y), grp: 16 (over z, x, core).
Axes of the slice: x: 2, y: 2, z: 4, core: 2. Of those that a mesh axis runs over, the one named last changes fastest.
Arguments:
- tokens: bfloat16 [2, 256, 7168], P(None, ('rep', 'grp')), parts along dimension 1, may hold values from -6 to 6
- expert_ids: int32 [2, 256, 4], P(None, ('rep', 'grp')), parts along dimension 1, may hold values from 0 to 15, as said below
- gate_weights: bfloat16 [2, 256, 4], P(None, ('rep', 'grp')), parts along dimension 1, may hold values from 0.099609375 to 1
- w_gate: bfloat16 [16, 7168, 2048], P('grp'), may hold values from -0.0625 to 0.0625
- w_up: bfloat16 [16, 7168, 2048], P('grp'), may hold values from -0.0625 to 0.0625
- w_down: bfloat16 [16, 2048, 7168], P('grp'), may hold values from -0.125 to 0.125
Outputs:
- mixed: bfloat16 [2, 256, 7168], P(None, ('rep', 'grp')), parts along dimension 1
The draws below stay inside these ranges and needn't reach their ends.
There are 2 independent parts, one for each index of `rep`. The reference program is written for one: setup_inputs(seed, part) draws one part's arguments, and reference() takes and returns one part's arrays. A program takes and returns all parts, laid end to end along the dimension named above; an argument that names none is the same for every part. Nothing has to cross between parts.
Inputs may be any that keep to these rules, and one draw needn't show every extreme that they name: `expert_ids`: A row's 4 ids are distinct and lie in two to four groups. In each micro-batch, at most 4 of one device's 8 rows route to any one group, and on every device some group receives exactly 4 of them.
All inputs are finite; a program needn't handle non-finite values.
Results may differ from the reference program's by a relative error of at most 0.006.
Values may be sent and summed in bfloat16 or wider, within the bound.
No kernel may reach another device: no remote copies, remote signals or barrier semaphores. Data moves between devices by JAX's collectives and lax.ppermute only.
A program may use at most 192 MiB of HBM per device.

```python
import math
import jax
import jax.numpy as jnp
from jax import lax

D = 7168
FF = 2048
GROUPS = 8
EXP_GRP = 2
TOPK = 4
MB = 2
ROWS = 8
CAP = 4
HID = 2048
TOKENS = 128
N_GRP = 16


def draw_expert_ids(key, part):
    key = jax.random.fold_in(key, 7)
    blocks = MB * TOKENS // GROUPS
    key_perm, key_count, key_pick = jax.random.split(key, 3)
    orders = jax.vmap(lambda k: jax.random.permutation(k, GROUPS))(jax.random.split(key_perm, blocks)).astype(jnp.int32)
    lane = jnp.arange(GROUPS, dtype=jnp.int32)
    counts = jax.random.randint(key_count, (blocks, GROUPS), 2, 5)
    counts = jnp.where(lane[None, :] < 4, 4, counts)
    picks = jax.random.randint(key_pick, (blocks, GROUPS, 4), 0, EXP_GRP)
    chosen = []
    for step in range(4):
        where_at = jnp.broadcast_to((lane[None, :] + step) % GROUPS, (blocks, GROUPS))
        chosen.append(jnp.take_along_axis(orders, where_at, axis=1))
    four = [chosen[j] * EXP_GRP + picks[..., j] for j in range(4)]
    three = [chosen[0] * EXP_GRP, chosen[0] * EXP_GRP + 1, chosen[1] * EXP_GRP + picks[..., 1], chosen[2] * EXP_GRP + picks[..., 2]]
    two = [chosen[0] * EXP_GRP, chosen[0] * EXP_GRP + 1, chosen[1] * EXP_GRP, chosen[1] * EXP_GRP + 1]
    columns = []
    for j in range(4):
        columns.append(jnp.where(counts == 4, four[j], jnp.where(counts == 3, three[j], two[j])))
    result = jnp.stack(columns, axis=-1).astype(jnp.int32)
    return result.reshape(MB, TOKENS, TOPK)


def block_scale(key, shape, cuts, smallest, largest):
    level, own = 1.0, jax.random.fold_in(key, 6)
    for position, parts in cuts:
        heights = jnp.exp(jax.random.uniform(jax.random.fold_in(own, position), (parts,), jnp.float32, smallest / len(cuts), largest / len(cuts)))
        level = level * jnp.repeat(heights, shape[position] // parts).reshape([-1 if axis == position else 1 for axis in range(len(shape))])
    return level


def scatter_about(rng, shape, width, limit, shards=(), held_as=jnp.bfloat16):
    entries = jax.random.normal(rng, shape, jnp.float32) * width
    if len(shards) > 0:
        entries = block_scale(rng, shape, shards, -0.22, 0.18) * entries
    return jnp.clip(entries, min=-limit, max=limit).astype(held_as)


def setup_inputs(seed: int = 0, part: int = 0) -> dict:
    seeds = jax.random.split(jax.random.key(seed), 7)
    own_keys = jax.random.split(jax.random.fold_in(seeds[6], part), 7)
    tokens = scatter_about(own_keys[0], (MB, TOKENS, D), 1.0, 6.0, ((1, 16),))
    expert_ids = draw_expert_ids(jax.random.fold_in(jax.random.fold_in(seeds[6], part), 71), part)
    gate_weights = jnp.clip(jnp.exp(math.log(1.0) - 2.306499 * jax.random.uniform(own_keys[2], (MB, TOKENS, TOPK), jnp.float32) ** block_scale(own_keys[2], (MB, TOKENS, TOPK), ((1, 16),), -0.2, 0.2)), 0.099609375, 1.0).astype(jnp.bfloat16)
    w_gate = scatter_about(seeds[3], (N_GRP, D, HID), D ** -0.5, 0.0625, ((0, 16),))
    w_up = scatter_about(seeds[4], (N_GRP, D, HID), D ** -0.5, 0.0625, ((0, 16),))
    w_down = scatter_about(seeds[5], (N_GRP, HID, D), FF ** -0.5, 0.125, ((0, 16),))
    return {"tokens": tokens, "expert_ids": expert_ids, "gate_weights": gate_weights, "w_gate": w_gate, "w_up": w_up, "w_down": w_down}


def reference(tokens, expert_ids, gate_weights, w_gate, w_up, w_down):
    gsize = N_GRP // GROUPS
    per_expert = gsize // EXP_GRP
    x = tokens.reshape(MB, N_GRP, ROWS, D)
    ids = expert_ids.reshape(MB, N_GRP, ROWS, TOPK)
    weights = gate_weights.reshape(MB, N_GRP, ROWS, TOPK).astype(jnp.float32)
    owner = ids // EXP_GRP
    group_grid = jnp.arange(GROUPS, dtype=jnp.int32)
    routed = jnp.any(owner[..., None, :] == group_grid[:, None], axis=-1)
    routed_int = routed.astype(jnp.int32)
    slots = jnp.cumsum(routed_int, axis=2) - routed_int
    slot_grid = jnp.arange(CAP, dtype=jnp.int32)
    dispatch = jnp.logical_and(routed[..., None], slots[..., None] == slot_grid).astype(jnp.float32)
    expert_grid = group_grid[:, None] * EXP_GRP + jnp.arange(EXP_GRP, dtype=jnp.int32)[None, :]
    local_weight = jnp.sum(jnp.where(ids[..., None, None, :] == expert_grid[..., None], weights[..., None, None, :], 0.0), axis=-1)
    bucket = jnp.einsum('bnrtc,bnrd->tbncd', dispatch, x.astype(jnp.float32)).astype(jnp.bfloat16)
    bucket_weight = jnp.einsum('bnrtc,bnrte->tbnce', dispatch, local_weight)
    gate_all = w_gate.reshape(GROUPS, gsize, D, HID)
    up_all = w_up.reshape(GROUPS, gsize, D, HID)
    down_all = w_down.reshape(GROUPS, gsize, HID, D)
    slice_expert = (jnp.arange(gsize, dtype=jnp.int32) // per_expert).astype(jnp.int32)
    expert_lane = jnp.arange(EXP_GRP, dtype=jnp.int32)

    def group_fn(items):
        rows, row_weight, gate_w, up_w, down_w = items
        flat_rows = rows.reshape(-1, D)
        flat_weight = row_weight.reshape(-1, EXP_GRP).astype(jnp.float32)

        def slice_fn(total, pieces):
            gate_s, up_s, down_s, expert = pieces
            select = (expert_lane == expert).astype(jnp.float32)
            column = jnp.sum(flat_weight * select[None, :], axis=1, keepdims=True)
            gate = jnp.dot(flat_rows, gate_s, preferred_element_type=jnp.float32)
            up = jnp.dot(flat_rows, up_s, preferred_element_type=jnp.float32)
            hidden = (jax.nn.silu(gate) * up * column).astype(jnp.bfloat16)
            part = jnp.dot(hidden, down_s, preferred_element_type=jnp.float32)
            rounded = lax.optimization_barrier(part.astype(jnp.bfloat16))
            return total + rounded.astype(jnp.float32), None

        start = jnp.zeros((flat_rows.shape[0], D), jnp.float32)
        total, _ = lax.scan(slice_fn, start, (gate_w, up_w, down_w, slice_expert))
        return total.astype(jnp.bfloat16).reshape(rows.shape)

    results = lax.map(group_fn, (bucket, bucket_weight, gate_all, up_all, down_all))
    mixed = jnp.einsum('bnrtc,tbncd->bnrd', dispatch, results.astype(jnp.float32))
    return mixed.astype(jnp.bfloat16).reshape(MB, TOKENS, D)
```

```python
import jax
import jax.numpy as jnp
from jax import lax
from jax.sharding import PartitionSpec as P

GROUPS = 8
EXP_GRP = 2
EXTRA = 128
IN_CUTS = 1
OUT_CUTS = 1


def exchanged(shard, by, unit):
    size = lax.axis_size("grp")
    return lax.ppermute(
        shard, "grp", [(i, ((i // unit) ^ by) * unit + i % unit) for i in range(size)]
    )


def spans(width, cuts):
    step = width // cuts
    return [(k * step, step) for k in range(cuts)]


def body(tokens, expert_ids, gate_weights, w_gate, w_up, w_down):
    devices = lax.axis_size("grp")
    gsize = devices // GROUPS
    in_bits = gsize.bit_length() - 1
    rank = lax.axis_index("grp")
    group_me = rank // gsize
    my_expert = group_me * EXP_GRP + rank % gsize // (gsize // EXP_GRP)
    batches, rows, width = tokens.shape
    cap = rows // 2
    topk = expert_ids.shape[2]
    block = batches * cap

    targets = group_me ^ jnp.arange(GROUPS, dtype=jnp.int32)
    routed = jnp.any(
        (expert_ids // EXP_GRP)[:, :, None, :] == targets[None, None, :, None], axis=-1
    )
    routed_int = routed.astype(jnp.int32)
    slots = jnp.cumsum(routed_int, axis=1) - routed_int
    dispatch = jnp.logical_and(
        routed[..., None], slots[..., None] == jnp.arange(cap, dtype=jnp.int32)
    )
    same = jnp.eye(batches, dtype=bool)
    slot_rows = (
        jnp.logical_and(
            dispatch.transpose(2, 0, 3, 1)[:, :, :, None, :], same[None, :, None, :, None]
        )
        .astype(jnp.bfloat16)
        .reshape(GROUPS * block, batches * rows)
    )

    flat = tokens.reshape(batches * rows, width)
    extra = jnp.concatenate(
        [
            expert_ids.astype(jnp.bfloat16).reshape(batches * rows, topk),
            gate_weights.reshape(batches * rows, topk),
            jnp.zeros((batches * rows, EXTRA - 2 * topk), jnp.bfloat16),
        ],
        axis=1,
    )

    gate = up_val = column = None
    for k, (at, step) in enumerate(spans(width, IN_CUTS)):
        part = flat[:, at : at + step]
        if k == 0:
            part = jnp.concatenate([part, extra], axis=1)
        bucket = jnp.dot(slot_rows, part, preferred_element_type=jnp.float32).astype(jnp.bfloat16)
        arrived = [bucket[:block]]
        for by in range(1, GROUPS):
            arrived.append(exchanged(bucket[by * block : (by + 1) * block], by, gsize))
        all_rows = jnp.concatenate(arrived)
        for bit in range(in_bits):
            all_rows = jnp.concatenate([all_rows, exchanged(all_rows, 1 << bit, 1)])
        if k == 0:
            ids = all_rows[:, step : step + topk]
            weights = all_rows[:, step + topk : step + 2 * topk].astype(jnp.float32)
            chosen = ids == my_expert.astype(jnp.bfloat16)
            column = jnp.sum(jnp.where(chosen, weights, 0.0), axis=1, keepdims=True)
            all_rows = all_rows[:, :step]
        gate_k = jnp.dot(all_rows, w_gate[0, at : at + step], preferred_element_type=jnp.float32)
        up_k = jnp.dot(all_rows, w_up[0, at : at + step], preferred_element_type=jnp.float32)
        gate = gate_k if gate is None else gate + gate_k
        up_val = up_k if up_val is None else up_val + up_k
    hidden = (jax.nn.silu(gate) * up_val * column).astype(jnp.bfloat16)

    outputs = []
    for at, step in spans(width, OUT_CUTS):
        total = jnp.dot(hidden, w_down[0, :, at : at + step], preferred_element_type=jnp.float32)
        for bit in reversed(range(in_bits)):
            half = total.shape[0] // 2
            got = exchanged(total[half:].astype(jnp.bfloat16), 1 << bit, 1)
            total = total[:half] + got.astype(jnp.float32)
        result = total.astype(jnp.bfloat16)
        back = [result[:block]]
        for by in range(1, GROUPS):
            back.append(exchanged(result[by * block : (by + 1) * block], by, gsize))
        mixed = lax.dot_general(
            slot_rows,
            jnp.concatenate(back),
            (((0,), (0,)), ((), ())),
            preferred_element_type=jnp.float32,
        )
        outputs.append(mixed.astype(jnp.bfloat16))
    return jnp.concatenate(outputs, axis=1).reshape(batches, rows, width)


def solution(mesh):
    split = P(None, ("rep", "grp"), None)
    stacked = P("grp", None, None)
    return jax.shard_map(
        body,
        mesh=mesh,
        in_specs=(split, split, split, stacked, stacked, stacked),
        out_specs=split,
        check_vma=False,
    )
```

```python
import functools

import jax
import jax.numpy as jnp
from jax import lax
from jax.experimental import pallas as pl
from jax.experimental.pallas import tpu as pltpu
from jax.sharding import PartitionSpec as P

GROUPS = 8
EXP_GRP = 2
EXTRA = 128
IN_CUTS = 2
OUT_CUTS = 2
DEPTH = 512
COLUMNS = 512
VMEM = 24 << 20


def exchanged(shard, by, unit):
    size = lax.axis_size("grp")
    return lax.ppermute(
        shard, "grp", [(i, ((i // unit) ^ by) * unit + i % unit) for i in range(size)]
    )


def spans(width, cuts):
    step = width // cuts
    return [(k * step, step) for k in range(cuts)]


def call(kernel, out_shape, cost, **kwargs):
    flops, moved = cost
    return pl.pallas_call(
        kernel,
        out_shape=out_shape,
        compiler_params=pltpu.CompilerParams(vmem_limit_bytes=VMEM),
        cost_estimate=pl.CostEstimate(flops=flops, bytes_accessed=moved, transcendentals=0),
        **kwargs,
    )


def bf16(*shape):
    return jax.ShapeDtypeStruct(shape, jnp.bfloat16)


def f32(*shape):
    return jax.ShapeDtypeStruct(shape, jnp.float32)


def iota(shape, dim):
    return lax.broadcasted_iota(jnp.int32, shape, dim)


def slot_matrix(group_me, ids, batches, rows):
    cap = rows // 2
    count = batches * rows
    block = batches * cap
    eye = (iota((count, count), 0) == iota((count, count), 1)).astype(jnp.float32)
    across = lax.dot_general(ids, eye, (((0,), (0,)), ((), ())), preferred_element_type=jnp.float32)
    across = across.astype(jnp.int32)
    shape = (GROUPS * block, count)
    where = iota(shape, 0)
    lane = iota(shape, 1)
    target = group_me ^ (where // block)
    routed = jnp.zeros(shape, jnp.float32)
    for k in range(ids.shape[1]):
        routed = jnp.where(across[k : k + 1, :] // EXP_GRP == target, 1.0, routed)
    above, here = iota((count, count), 0), iota((count, count), 1)
    before = jnp.where((above < here) & (above // rows == here // rows), 1.0, 0.0)
    slots = jnp.dot(routed, before, preferred_element_type=jnp.float32).astype(jnp.int32)
    taken = (slots == where % cap) & (lane // rows == where % block // cap)
    return jnp.where(taken, routed, 0.0).astype(jnp.bfloat16)


def prep_kernel(cuts, group_ref, tokens_ref, ids_ref, weights_ref, matrix_ref, *out_refs):
    batches, rows, width = tokens_ref.shape
    count = batches * rows
    ids = ids_ref[...].reshape(count, ids_ref.shape[2]).astype(jnp.float32)
    weights = weights_ref[...].astype(jnp.float32).reshape(count, ids_ref.shape[2])
    matrix = slot_matrix(group_ref[0], ids, batches, rows)
    matrix_ref[...] = matrix
    block = matrix.shape[0] // GROUPS
    topk = ids.shape[1]
    for k, (at, step) in enumerate(spans(width, cuts)):
        part = tokens_ref[:, :, at : at + step].reshape(count, step)
        bucket = jnp.dot(matrix, part, preferred_element_type=jnp.float32)
        if k == 0:
            extra = jnp.concatenate(
                [ids, weights, jnp.zeros((count, EXTRA - 2 * topk), jnp.float32)], axis=1
            ).astype(jnp.bfloat16)
            more = jnp.dot(matrix, extra, preferred_element_type=jnp.float32)
        for t in range(GROUPS):
            out = out_refs[k * GROUPS + t]
            out[:, :step] = bucket[t * block : (t + 1) * block].astype(jnp.bfloat16)
            if k == 0:
                out[:, step:] = more[t * block : (t + 1) * block].astype(jnp.bfloat16)


def join_kernel(*refs):
    refs[-1][...] = jnp.concatenate(
        [r[...].astype(jnp.float32) for r in refs[:-1]], axis=0
    ).astype(jnp.bfloat16)


def up_kernel(parts, first, last, topk, expert_ref, *refs):
    x = jnp.concatenate([r[...] for r in refs[:parts]], axis=0)
    refs = refs[parts:]
    extras, refs = refs[:parts], refs[parts:]
    w_gate_ref, w_up_ref, refs = refs[0], refs[1], refs[2:]
    if not first:
        gate_in, up_in, refs = refs[0], refs[1], refs[2:]
    if last:
        hidden_ref, gate_acc, up_acc = refs
    else:
        gate_acc, up_acc = refs
    i = pl.program_id(0)

    @pl.when(i == 0)
    def _():
        gate_acc[...] = jnp.zeros_like(gate_acc) if first else gate_in[...]
        up_acc[...] = jnp.zeros_like(up_acc) if first else up_in[...]

    gate_acc[...] += jnp.dot(x, w_gate_ref[0], preferred_element_type=jnp.float32)
    up_acc[...] += jnp.dot(x, w_up_ref[0], preferred_element_type=jnp.float32)

    if last:

        @pl.when(i == pl.num_programs(0) - 1)
        def _():
            extra = jnp.concatenate([r[...].astype(jnp.float32) for r in extras], axis=0)
            expert = expert_ref[0].astype(jnp.float32)
            column = jnp.zeros((extra.shape[0], 1), jnp.float32)
            for k in range(topk):
                column += jnp.where(
                    extra[:, k : k + 1] == expert, extra[:, topk + k : topk + k + 1], 0.0
                )
            gate = gate_acc[...]
            hidden_ref[...] = (jax.nn.silu(gate) * up_acc[...] * column).astype(jnp.bfloat16)


def down_kernel(hidden_ref, w_ref, kept_ref, away_ref):
    total = jnp.dot(hidden_ref[...], w_ref[0], preferred_element_type=jnp.float32)
    half = kept_ref.shape[0]
    kept_ref[...] = total[:half].astype(jnp.bfloat16)
    away_ref[...] = total[half:].astype(jnp.bfloat16)


def sum_kernel(kept_ref, got_ref, *out_refs):
    total = kept_ref[...].astype(jnp.float32) + got_ref[...].astype(jnp.float32)
    block = out_refs[0].shape[0]
    for t, out in enumerate(out_refs):
        out[...] = total[t * block : (t + 1) * block].astype(jnp.bfloat16)


def mix_kernel(cuts, matrix_ref, *refs):
    out_ref = refs[-1]
    batches, rows, width = out_ref.shape
    for k, (at, step) in enumerate(spans(width, cuts)):
        back = jnp.concatenate(
            [r[...].astype(jnp.float32) for r in refs[k * GROUPS : (k + 1) * GROUPS]], axis=0
        ).astype(jnp.bfloat16)
        mixed = lax.dot_general(
            matrix_ref[...], back, (((0,), (0,)), ((), ())), preferred_element_type=jnp.float32
        )
        for b in range(batches):
            out_ref[b, :, at : at + step] = mixed[b * rows : (b + 1) * rows].astype(jnp.bfloat16)


def body(tokens, expert_ids, gate_weights, w_gate, w_up, w_down):
    devices = lax.axis_size("grp")
    gsize = devices // GROUPS
    in_bits = gsize.bit_length() - 1
    rank = lax.axis_index("grp")
    group_me = (rank // gsize).astype(jnp.int32)
    my_expert = (group_me * EXP_GRP + rank % gsize // (gsize // EXP_GRP)).astype(jnp.int32)
    batches, rows, width = tokens.shape
    cap = rows // 2
    topk = expert_ids.shape[2]
    block = batches * cap
    hid = w_gate.shape[2]
    total_rows = gsize * GROUPS * block
    smem = pl.BlockSpec(memory_space=pltpu.SMEM)
    vmem = pl.BlockSpec(memory_space=pltpu.VMEM)

    in_spans = spans(width, IN_CUTS)
    widths = [step + (EXTRA if k == 0 else 0) for k, (_, step) in enumerate(in_spans)]
    matrix, *buckets = call(
        functools.partial(prep_kernel, IN_CUTS),
        [bf16(GROUPS * block, batches * rows)]
        + [bf16(block, w) for w in widths for _ in range(GROUPS)],
        (2 * GROUPS * block * batches * rows * width, 2 * 5 * batches * rows * width),
        in_specs=[smem, vmem, vmem, vmem],
        out_specs=[vmem] * (1 + GROUPS * IN_CUTS),
    )(group_me.reshape(1), tokens, expert_ids, gate_weights)

    arrived = []
    for k in range(IN_CUTS):
        mine = buckets[k * GROUPS : (k + 1) * GROUPS]
        arrived.append([mine[0]] + [exchanged(mine[by], by, gsize) for by in range(1, GROUPS)])

    first_parts = None
    gate_up = ()
    for k, (at, step) in enumerate(in_spans):
        parts = [
            call(
                join_kernel,
                bf16(GROUPS * block, widths[k]),
                (0, 4 * GROUPS * block * widths[k]),
                in_specs=[vmem] * GROUPS,
                out_specs=vmem,
            )(*arrived[k])
        ]
        for bit in range(in_bits):
            all_rows = parts[0] if bit == 0 else jnp.concatenate(parts)
            parts.append(exchanged(all_rows, 1 << bit, 1))
        if k == 0:
            first_parts = parts
        last = k == IN_CUTS - 1
        depth = DEPTH if step % DEPTH == 0 else step // 7
        acc = pl.BlockSpec((total_rows, hid), lambda i: (0, 0))
        weight = pl.BlockSpec((1, depth, hid), lambda i, at=at, depth=depth: (0, at // depth + i, 0))
        outs = call(
            functools.partial(up_kernel, len(parts), k == 0, last, topk),
            bf16(total_rows, hid) if last else [f32(total_rows, hid)] * 2,
            (4 * total_rows * step * hid, 4 * step * hid),
            grid=(step // depth,),
            in_specs=[smem]
            + [pl.BlockSpec((p.shape[0], depth), lambda i: (0, i)) for p in parts]
            + [
                pl.BlockSpec((p.shape[0], EXTRA), lambda i: (0, in_spans[0][1] // EXTRA))
                for p in first_parts
            ]
            + [weight, weight]
            + ([] if k == 0 else [acc, acc]),
            out_specs=acc if last else [acc, acc],
            scratch_shapes=[pltpu.VMEM((total_rows, hid), jnp.float32)] * 2 if last else [],
        )(my_expert.reshape(1), *parts, *first_parts, w_gate, w_up, *gate_up)
        if last:
            hidden = outs
        else:
            gate_up = outs

    returned = []
    for at, step in spans(width, OUT_CUTS):
        half = total_rows // 2
        kept, away = call(
            down_kernel,
            [bf16(half, step)] * 2,
            (2 * total_rows * step * hid, 2 * step * hid),
            grid=(step // COLUMNS,),
            in_specs=[
                pl.BlockSpec((total_rows, hid), lambda j: (0, 0)),
                pl.BlockSpec((1, hid, COLUMNS), lambda j, at=at: (0, 0, at // COLUMNS + j)),
            ],
            out_specs=[pl.BlockSpec((half, COLUMNS), lambda j: (0, j))] * 2,
        )(hidden, w_down)
        got = exchanged(away, 1 << (in_bits - 1), 1)
        for bit in reversed(range(in_bits - 1)):
            total = kept.astype(jnp.float32) + got.astype(jnp.float32)
            half = total.shape[0] // 2
            kept = total[:half].astype(jnp.bfloat16)
            got = exchanged(total[half:].astype(jnp.bfloat16), 1 << bit, 1)
        results = call(
            sum_kernel,
            [bf16(block, step)] * GROUPS,
            (0, 6 * GROUPS * block * step),
            in_specs=[vmem, vmem],
            out_specs=[vmem] * GROUPS,
        )(kept, got)
        returned += [results[0]] + [exchanged(results[by], by, gsize) for by in range(1, GROUPS)]

    return call(
        functools.partial(mix_kernel, OUT_CUTS),
        bf16(batches, rows, width),
        (2 * GROUPS * block * batches * rows * width, 2 * 5 * batches * rows * width),
        in_specs=[vmem] * (1 + GROUPS * OUT_CUTS),
        out_specs=vmem,
    )(matrix, *returned)


def solution(mesh):
    split = P(None, ("rep", "grp"), None)
    stacked = P("grp", None, None)
    return jax.shard_map(
        body,
        mesh=mesh,
        in_specs=(split, split, split, stacked, stacked, stacked),
        out_specs=split,
        check_vma=False,
    )
```

```python
import functools

import jax
import jax.numpy as jnp
from jax import lax
from jax.experimental import pallas as pl
from jax.experimental.pallas import tpu as pltpu
from jax.sharding import PartitionSpec as P

GROUPS = 8
EXP_GRP = 2
EXTRA = 128
DEPTH = 512
COLUMNS = 512
AHEAD = 4


def exchanged(shard, by, unit):
    size = lax.axis_size("grp")
    return lax.ppermute(
        shard, "grp", [(i, ((i // unit) ^ by) * unit + i % unit) for i in range(size)]
    )


def call(kernel, out_shape, cost, limit=16 << 20, **kwargs):
    flops, moved = cost
    return pl.pallas_call(
        kernel,
        out_shape=out_shape,
        compiler_params=pltpu.CompilerParams(vmem_limit_bytes=limit),
        cost_estimate=pl.CostEstimate(flops=flops, bytes_accessed=moved, transcendentals=0),
        **kwargs,
    )


def bf16(*shape):
    return jax.ShapeDtypeStruct(shape, jnp.bfloat16)


def f32(*shape):
    return jax.ShapeDtypeStruct(shape, jnp.float32)


def iota(shape, dim):
    return lax.broadcasted_iota(jnp.int32, shape, dim)


def slot_matrix(group_me, ids, batches, rows):
    cap = rows // 2
    count = batches * rows
    block = batches * cap
    eye = (iota((count, count), 0) == iota((count, count), 1)).astype(jnp.float32)
    across = lax.dot_general(ids, eye, (((0,), (0,)), ((), ())), preferred_element_type=jnp.float32)
    across = across.astype(jnp.int32)
    shape = (GROUPS * block, count)
    where = iota(shape, 0)
    lane = iota(shape, 1)
    target = group_me ^ (where // block)
    routed = jnp.zeros(shape, jnp.float32)
    for k in range(ids.shape[1]):
        routed = jnp.where(across[k : k + 1, :] // EXP_GRP == target, 1.0, routed)
    above, here = iota((count, count), 0), iota((count, count), 1)
    before = jnp.where((above < here) & (above // rows == here // rows), 1.0, 0.0)
    slots = jnp.dot(routed, before, preferred_element_type=jnp.float32).astype(jnp.int32)
    taken = (slots == where % cap) & (lane // rows == where % block // cap)
    return jnp.where(taken, routed, 0.0).astype(jnp.bfloat16)


def prep_kernel(topk, group_ref, tokens_ref, extra_ref, matrix_ref, *out_refs):
    batches, rows, width = tokens_ref.shape
    extra = extra_ref[...]
    matrix = slot_matrix(group_ref[0], extra[:, :topk].astype(jnp.float32), batches, rows)
    matrix_ref[...] = matrix
    block = matrix.shape[0] // GROUPS
    tokens = tokens_ref[...].reshape(batches * rows, width)
    bucket = jnp.dot(matrix, tokens, preferred_element_type=jnp.float32)
    more = jnp.dot(matrix, extra, preferred_element_type=jnp.float32)
    for t, out in enumerate(out_refs):
        out[:, :width] = bucket[t * block : (t + 1) * block].astype(jnp.bfloat16)
        out[:, width:] = more[t * block : (t + 1) * block].astype(jnp.bfloat16)


def join_kernel(*refs):
    refs[-1][...] = jnp.concatenate(
        [r[...].astype(jnp.float32) for r in refs[:-1]], axis=0
    ).astype(jnp.bfloat16)


def fetch_kernel(after_ref, w_ref, out_ref, sem):
    del after_ref
    copies = [
        pltpu.make_async_copy(
            w_ref.at[0, d : d + DEPTH], out_ref.at[d : d + DEPTH], sem.at[d // DEPTH]
        )
        for d in range(0, out_ref.shape[0], DEPTH)
    ]
    for copy in copies:
        copy.start()
    for copy in copies:
        copy.wait()


def expert_kernel(parts, topk, expert_ref, *refs):
    xs, refs = refs[:parts], refs[parts:]
    w_gate_ref, w_up_ref, w_down_ref, kept_ref, away_ref = refs[:5]
    gate_acc, up_acc, hidden, up_slots, up_sem, down_slots, down_sem = refs[5:]
    half, width = kept_ref.shape
    ups, downs = width // DEPTH, width // COLUMNS
    copies = [
        pltpu.make_async_copy(
            w_up_ref.at[0, i * DEPTH : (i + 1) * DEPTH],
            up_slots.at[i % AHEAD],
            up_sem.at[i % AHEAD],
        )
        for i in range(ups)
    ] + [
        pltpu.make_async_copy(
            w_down_ref.at[0, :, j * COLUMNS : (j + 1) * COLUMNS],
            down_slots.at[j % AHEAD],
            down_sem.at[j % AHEAD],
        )
        for j in range(downs)
    ]
    for copy in copies[:AHEAD]:
        copy.start()

    for i in range(ups):
        here = slice(i * DEPTH, (i + 1) * DEPTH)
        x = jnp.concatenate([r[:, here] for r in xs], axis=0)
        gate = jnp.dot(x, w_gate_ref[here], preferred_element_type=jnp.float32)
        if i == 0:
            gate_acc[...] = gate
        else:
            gate_acc[...] += gate
        copies[i].wait()
        up = jnp.dot(x, up_slots[i % AHEAD], preferred_element_type=jnp.float32)
        if i == 0:
            up_acc[...] = up
        else:
            up_acc[...] += up
        copies[i + AHEAD].start()

    extra = jnp.concatenate([r[:, width:].astype(jnp.float32) for r in xs], axis=0)
    expert = expert_ref[0].astype(jnp.float32)
    column = jnp.zeros((extra.shape[0], 1), jnp.float32)
    for k in range(topk):
        column += jnp.where(
            extra[:, k : k + 1] == expert, extra[:, topk + k : topk + k + 1], 0.0
        )
    hidden[...] = (jax.nn.silu(gate_acc[...]) * up_acc[...] * column).astype(jnp.bfloat16)

    for j in range(downs):
        copies[ups + j].wait()
        total = jnp.dot(hidden[...], down_slots[j % AHEAD], preferred_element_type=jnp.float32)
        here = slice(j * COLUMNS, (j + 1) * COLUMNS)
        kept_ref[:, here] = total[:half].astype(jnp.bfloat16)
        away_ref[:, here] = total[half:].astype(jnp.bfloat16)
        if j + AHEAD < downs:
            copies[ups + j + AHEAD].start()


def sum_kernel(kept_ref, got_ref, *out_refs):
    total = kept_ref[...].astype(jnp.float32) + got_ref[...].astype(jnp.float32)
    block = out_refs[0].shape[0]
    for t, out in enumerate(out_refs):
        out[...] = total[t * block : (t + 1) * block].astype(jnp.bfloat16)


def mix_kernel(matrix_ref, *refs):
    out_ref = refs[-1]
    batches, rows, width = out_ref.shape
    back = jnp.concatenate([r[...].astype(jnp.float32) for r in refs[:-1]], axis=0)
    mixed = lax.dot_general(
        matrix_ref[...],
        back.astype(jnp.bfloat16),
        (((0,), (0,)), ((), ())),
        preferred_element_type=jnp.float32,
    )
    for b in range(batches):
        out_ref[b] = mixed[b * rows : (b + 1) * rows].astype(jnp.bfloat16)


def body(tokens, expert_ids, gate_weights, w_gate, w_up, w_down):
    devices = lax.axis_size("grp")
    gsize = devices // GROUPS
    in_bits = gsize.bit_length() - 1
    rank = lax.axis_index("grp")
    group_me = (rank // gsize).astype(jnp.int32)
    my_expert = (group_me * EXP_GRP + rank % gsize // (gsize // EXP_GRP)).astype(jnp.int32)
    batches, rows, width = tokens.shape
    count = batches * rows
    topk = expert_ids.shape[2]
    block = batches * (rows // 2)
    hid = w_gate.shape[2]
    total_rows = gsize * GROUPS * block
    half = total_rows // 2
    wide = width + EXTRA
    smem = pl.BlockSpec(memory_space=pltpu.SMEM)
    vmem = pl.BlockSpec(memory_space=pltpu.VMEM)
    hbm = pl.BlockSpec(memory_space=pl.ANY)

    def to_all(blocks):
        got = {by: exchanged(blocks[by], by, gsize) for by in reversed(range(1, GROUPS))}
        return [blocks[0]] + [got[by] for by in range(1, GROUPS)]

    extra = jnp.concatenate(
        [
            expert_ids.astype(jnp.bfloat16),
            gate_weights,
            jnp.zeros((batches, rows, EXTRA - 2 * topk), jnp.bfloat16),
        ],
        axis=2,
    ).reshape(count, EXTRA)
    matrix, *buckets = call(
        functools.partial(prep_kernel, topk),
        [bf16(GROUPS * block, count)] + [bf16(block, wide)] * GROUPS,
        (2 * GROUPS * block * count * wide, 10 * count * wide),
        in_specs=[smem, vmem, vmem],
        out_specs=[vmem] * (1 + GROUPS),
    )(group_me.reshape(1), tokens, extra)
    fetched = call(
        fetch_kernel,
        pltpu.VMEM((width, hid), jnp.bfloat16),
        (0, 4 * width * hid),
        in_specs=[hbm, hbm],
        out_specs=vmem,
        scratch_shapes=[pltpu.SemaphoreType.DMA((width // DEPTH,))],
    )(matrix, w_gate)
    fetched = pltpu.with_memory_space_constraint(fetched, pltpu.VMEM)
    parts = [
        call(
            join_kernel,
            bf16(GROUPS * block, wide),
            (0, 4 * GROUPS * block * wide),
            in_specs=[vmem] * GROUPS,
            out_specs=vmem,
        )(*to_all(buckets))
    ]
    for bit in range(in_bits):
        all_rows = parts[0] if bit == 0 else jnp.concatenate(parts)
        parts.append(exchanged(all_rows, 1 << bit, 1))

    slots = 2 * AHEAD * max(DEPTH, COLUMNS) * hid * 2
    kept, away = call(
        functools.partial(expert_kernel, len(parts), topk),
        [bf16(half, width)] * 2,
        (6 * total_rows * width * hid, 4 * width * hid),
        limit=slots + total_rows * (10 * hid + 4 * wide) + (6 << 20),
        in_specs=[smem] + [vmem] * (len(parts) + 1) + [hbm, hbm],
        out_specs=[vmem] * 2,
        scratch_shapes=[
            pltpu.VMEM((total_rows, hid), jnp.float32),
            pltpu.VMEM((total_rows, hid), jnp.float32),
            pltpu.VMEM((total_rows, hid), jnp.bfloat16),
            pltpu.VMEM((AHEAD, DEPTH, hid), jnp.bfloat16),
            pltpu.SemaphoreType.DMA((AHEAD,)),
            pltpu.VMEM((AHEAD, hid, COLUMNS), jnp.bfloat16),
            pltpu.SemaphoreType.DMA((AHEAD,)),
        ],
    )(my_expert.reshape(1), *parts, fetched, w_up, w_down)

    got = exchanged(away, 1 << (in_bits - 1), 1)
    for bit in reversed(range(in_bits - 1)):
        total = kept.astype(jnp.float32) + got.astype(jnp.float32)
        quarter = total.shape[0] // 2
        kept = total[:quarter].astype(jnp.bfloat16)
        got = exchanged(total[quarter:].astype(jnp.bfloat16), 1 << bit, 1)
    results = call(
        sum_kernel,
        [bf16(block, width)] * GROUPS,
        (0, 6 * GROUPS * block * width),
        in_specs=[vmem, vmem],
        out_specs=[vmem] * GROUPS,
    )(kept, got)

    return call(
        mix_kernel,
        bf16(batches, rows, width),
        (2 * GROUPS * block * count * width, 10 * count * width),
        in_specs=[vmem] * (1 + GROUPS),
        out_specs=vmem,
    )(matrix, *to_all(results))


def solution(mesh):
    split = P(None, ("rep", "grp"), None)
    stacked = P("grp", None, None)
    return jax.shard_map(
        body,
        mesh=mesh,
        in_specs=(split, split, split, stacked, stacked, stacked),
        out_specs=split,
        check_vma=False,
    )
```

```python
import functools

import jax
import jax.numpy as jnp
from jax import lax
from jax.experimental import pallas as pl
from jax.experimental.pallas import tpu as pltpu
from jax.sharding import PartitionSpec as P

GROUPS = 8
EXP_GRP = 2
EXTRA = 128
DEPTH = 512
COLUMNS = 512
AHEAD = 4
SMALL = 8 << 20
SLACK = 1 << 20
FETCHED = 3


def exchanged(shard, by, unit):
    size = lax.axis_size("grp")
    return lax.ppermute(
        shard, "grp", [(i, ((i // unit) ^ by) * unit + i % unit) for i in range(size)]
    )


def call(kernel, out_shape, cost, limit=SMALL, **kwargs):
    flops, moved = cost
    return pl.pallas_call(
        kernel,
        out_shape=out_shape,
        compiler_params=pltpu.CompilerParams(vmem_limit_bytes=limit),
        cost_estimate=pl.CostEstimate(flops=flops, bytes_accessed=moved, transcendentals=0),
        **kwargs,
    )


def bf16(*shape):
    return jax.ShapeDtypeStruct(shape, jnp.bfloat16)


def f32(*shape):
    return jax.ShapeDtypeStruct(shape, jnp.float32)


def iota(shape, dim):
    return lax.broadcasted_iota(jnp.int32, shape, dim)


def slot_matrix(group_me, ids, batches, rows):
    cap = rows // 2
    count = batches * rows
    block = batches * cap
    eye = (iota((count, count), 0) == iota((count, count), 1)).astype(jnp.float32)
    across = lax.dot_general(ids, eye, (((0,), (0,)), ((), ())), preferred_element_type=jnp.float32)
    across = across.astype(jnp.int32)
    shape = (GROUPS * block, count)
    where = iota(shape, 0)
    lane = iota(shape, 1)
    target = group_me ^ (where // block)
    routed = jnp.zeros(shape, jnp.float32)
    for k in range(ids.shape[1]):
        routed = jnp.where(across[k : k + 1, :] // EXP_GRP == target, 1.0, routed)
    above, here = iota((count, count), 0), iota((count, count), 1)
    before = jnp.where((above < here) & (above // rows == here // rows), 1.0, 0.0)
    slots = jnp.dot(routed, before, preferred_element_type=jnp.float32).astype(jnp.int32)
    taken = (slots == where % cap) & (lane // rows == where % block // cap)
    return jnp.where(taken, routed, 0.0).astype(jnp.bfloat16)


def prep_kernel(topk, group_ref, tokens_ref, extra_ref, matrix_ref, *out_refs):
    batches, rows, width = tokens_ref.shape
    extra = extra_ref[...]
    matrix = slot_matrix(group_ref[0], extra[:, :topk].astype(jnp.float32), batches, rows)
    matrix_ref[...] = matrix
    block = matrix.shape[0] // GROUPS
    tokens = tokens_ref[...].reshape(batches * rows, width)
    bucket = jnp.dot(matrix, tokens, preferred_element_type=jnp.float32)
    more = jnp.dot(matrix, extra, preferred_element_type=jnp.float32)
    for t, out in enumerate(out_refs):
        out[:, :width] = bucket[t * block : (t + 1) * block].astype(jnp.bfloat16)
        out[:, width:] = more[t * block : (t + 1) * block].astype(jnp.bfloat16)


def join_kernel(*refs):
    refs[-1][...] = jnp.concatenate(
        [r[...].astype(jnp.float32) for r in refs[:-1]], axis=0
    ).astype(jnp.bfloat16)


def fetch_kernel(after_ref, w_ref, out_ref, sem):
    del after_ref
    copies = [
        pltpu.make_async_copy(
            w_ref.at[0, d : d + DEPTH], out_ref.at[d : d + DEPTH], sem.at[d // DEPTH]
        )
        for d in range(0, out_ref.shape[0], DEPTH)
    ]
    for copy in copies:
        copy.start()
    for copy in copies:
        copy.wait()


def expert_kernel(parts, topk, expert_ref, *refs):
    xs, refs = refs[:parts], refs[parts:]
    w_gate_ref, w_rest_ref, w_up_ref, w_down_ref, kept_ref, away_ref = refs[:6]
    gate_acc, up_acc, hidden, up_slots, up_sem, down_slots, down_sem = refs[6:]
    half, width = kept_ref.shape
    ups, downs = width // DEPTH, width // COLUMNS
    held = w_gate_ref.shape[0] // DEPTH
    here = [slice(i * DEPTH, (i + 1) * DEPTH) for i in range(ups)]
    sources = []
    for i in range(ups):
        if i >= held:
            sources.append(w_rest_ref.at[0, here[i]])
        sources.append(w_up_ref.at[0, here[i]])
    count = len(sources)
    copies = [
        pltpu.make_async_copy(source, up_slots.at[n % AHEAD], up_sem.at[n % AHEAD])
        for n, source in enumerate(sources)
    ] + [
        pltpu.make_async_copy(
            w_down_ref.at[0, :, j * COLUMNS : (j + 1) * COLUMNS],
            down_slots.at[j % AHEAD],
            down_sem.at[j % AHEAD],
        )
        for j in range(downs)
    ]
    for copy in copies[:AHEAD]:
        copy.start()

    def add(acc, i, x, w):
        product = jnp.dot(x, w, preferred_element_type=jnp.float32)
        if i == 0:
            acc[...] = product
        else:
            acc[...] += product

    n = 0
    for i in range(ups):
        x = jnp.concatenate([r[:, here[i]] for r in xs], axis=0)
        if i < held:
            add(gate_acc, i, x, w_gate_ref[here[i]])
        for acc in [up_acc] if i < held else [gate_acc, up_acc]:
            copies[n].wait()
            add(acc, i, x, up_slots[n % AHEAD])
            copies[n + AHEAD].start()
            n += 1

    extra = jnp.concatenate([r[:, width:].astype(jnp.float32) for r in xs], axis=0)
    expert = expert_ref[0].astype(jnp.float32)
    column = jnp.zeros((extra.shape[0], 1), jnp.float32)
    for k in range(topk):
        column += jnp.where(
            extra[:, k : k + 1] == expert, extra[:, topk + k : topk + k + 1], 0.0
        )
    hidden[...] = (jax.nn.silu(gate_acc[...]) * up_acc[...] * column).astype(jnp.bfloat16)

    for j in range(downs):
        copies[count + j].wait()
        total = jnp.dot(hidden[...], down_slots[j % AHEAD], preferred_element_type=jnp.float32)
        at = slice(j * COLUMNS, (j + 1) * COLUMNS)
        kept_ref[:, at] = total[:half].astype(jnp.bfloat16)
        away_ref[:, at] = total[half:].astype(jnp.bfloat16)
        if j + AHEAD < downs:
            copies[count + j + AHEAD].start()


def sum_kernel(kept_ref, got_ref, *out_refs):
    total = kept_ref[...].astype(jnp.float32) + got_ref[...].astype(jnp.float32)
    block = out_refs[0].shape[0]
    for t, out in enumerate(out_refs):
        out[...] = total[t * block : (t + 1) * block].astype(jnp.bfloat16)


def mix_kernel(matrix_ref, *refs):
    out_ref = refs[-1]
    batches, rows, width = out_ref.shape
    back = jnp.concatenate([r[...].astype(jnp.float32) for r in refs[:-1]], axis=0)
    mixed = lax.dot_general(
        matrix_ref[...],
        back.astype(jnp.bfloat16),
        (((0,), (0,)), ((), ())),
        preferred_element_type=jnp.float32,
    )
    for b in range(batches):
        out_ref[b] = mixed[b * rows : (b + 1) * rows].astype(jnp.bfloat16)


def body(tokens, expert_ids, gate_weights, w_gate, w_up, w_down):
    devices = lax.axis_size("grp")
    gsize = devices // GROUPS
    in_bits = gsize.bit_length() - 1
    rank = lax.axis_index("grp")
    group_me = (rank // gsize).astype(jnp.int32)
    my_expert = (group_me * EXP_GRP + rank % gsize // (gsize // EXP_GRP)).astype(jnp.int32)
    batches, rows, width = tokens.shape
    count = batches * rows
    topk = expert_ids.shape[2]
    block = batches * (rows // 2)
    hid = w_gate.shape[2]
    total_rows = gsize * GROUPS * block
    half = total_rows // 2
    wide = width + EXTRA
    smem = pl.BlockSpec(memory_space=pltpu.SMEM)
    vmem = pl.BlockSpec(memory_space=pltpu.VMEM)
    hbm = pl.BlockSpec(memory_space=pl.ANY)

    def to_all(blocks):
        got = {by: exchanged(blocks[by], by, gsize) for by in reversed(range(1, GROUPS))}
        return [blocks[0]] + [got[by] for by in range(1, GROUPS)]

    extra = jnp.concatenate(
        [
            expert_ids.astype(jnp.bfloat16),
            gate_weights,
            jnp.zeros((batches, rows, EXTRA - 2 * topk), jnp.bfloat16),
        ],
        axis=2,
    ).reshape(count, EXTRA)
    matrix, *buckets = call(
        functools.partial(prep_kernel, topk),
        [bf16(GROUPS * block, count)] + [bf16(block, wide)] * GROUPS,
        (2 * GROUPS * block * count * wide, 10 * count * wide),
        in_specs=[smem, vmem, vmem],
        out_specs=[vmem] * (1 + GROUPS),
    )(group_me.reshape(1), tokens, extra)
    w_gate, w_up, w_down = (
        pltpu.with_memory_space_constraint(w, pltpu.HBM) for w in (w_gate, w_up, w_down)
    )
    fetched = call(
        fetch_kernel,
        pltpu.VMEM((FETCHED * DEPTH, hid), jnp.bfloat16),
        (0, 4 * FETCHED * DEPTH * hid),
        in_specs=[hbm, hbm],
        out_specs=vmem,
        scratch_shapes=[pltpu.SemaphoreType.DMA((FETCHED,))],
    )(matrix, w_gate)
    fetched = pltpu.with_memory_space_constraint(fetched, pltpu.VMEM)
    parts = [
        call(
            join_kernel,
            bf16(GROUPS * block, wide),
            (0, 4 * GROUPS * block * wide),
            in_specs=[vmem] * GROUPS,
            out_specs=vmem,
        )(*to_all(buckets))
    ]
    for bit in range(in_bits):
        all_rows = parts[0] if bit == 0 else jnp.concatenate(parts)
        parts.append(exchanged(all_rows, 1 << bit, 1))

    slots = 2 * AHEAD * max(DEPTH, COLUMNS) * hid * 2
    kept, away = call(
        functools.partial(expert_kernel, len(parts), topk),
        [bf16(half, width)] * 2,
        (6 * total_rows * width * hid, 4 * width * hid),
        limit=slots + total_rows * (10 * hid + 4 * wide) + SLACK,
        in_specs=[smem] + [vmem] * (len(parts) + 1) + [hbm] * 3,
        out_specs=[vmem] * 2,
        scratch_shapes=[
            pltpu.VMEM((total_rows, hid), jnp.float32),
            pltpu.VMEM((total_rows, hid), jnp.float32),
            pltpu.VMEM((total_rows, hid), jnp.bfloat16),
            pltpu.VMEM((AHEAD, DEPTH, hid), jnp.bfloat16),
            pltpu.SemaphoreType.DMA((AHEAD,)),
            pltpu.VMEM((AHEAD, hid, COLUMNS), jnp.bfloat16),
            pltpu.SemaphoreType.DMA((AHEAD,)),
        ],
    )(my_expert.reshape(1), *parts, fetched, w_gate, w_up, w_down)

    got = exchanged(away, 1 << (in_bits - 1), 1)
    for bit in reversed(range(in_bits - 1)):
        total = kept.astype(jnp.float32) + got.astype(jnp.float32)
        quarter = total.shape[0] // 2
        kept = total[:quarter].astype(jnp.bfloat16)
        got = exchanged(total[quarter:].astype(jnp.bfloat16), 1 << bit, 1)
    results = call(
        sum_kernel,
        [bf16(block, width)] * GROUPS,
        (0, 6 * GROUPS * block * width),
        in_specs=[vmem, vmem],
        out_specs=[vmem] * GROUPS,
    )(kept, got)

    return call(
        mix_kernel,
        bf16(batches, rows, width),
        (2 * GROUPS * block * count * width, 10 * count * width),
        in_specs=[vmem] * (1 + GROUPS),
        out_specs=vmem,
    )(matrix, *to_all(results))


def solution(mesh):
    split = P(None, ("rep", "grp"), None)
    stacked = P("grp", None, None)
    return jax.shard_map(
        body,
        mesh=mesh,
        in_specs=(split, split, split, stacked, stacked, stacked),
        out_specs=split,
        check_vma=False,
    )
```

```python
import functools

import jax
import jax.numpy as jnp
from jax import lax
from jax.experimental import pallas as pl
from jax.experimental.pallas import tpu as pltpu
from jax.sharding import PartitionSpec as P

GROUPS = 8
EXP_GRP = 2
EXTRA = 128
DEPTH = 512
COLUMNS = 512
AHEAD = 4
SMALL = 8 << 20
SLACK = 1 << 20
FETCHED = 3


def exchanged(shard, by, unit):
    size = lax.axis_size("grp")
    return lax.ppermute(
        shard, "grp", [(i, ((i // unit) ^ by) * unit + i % unit) for i in range(size)]
    )


def call(kernel, out_shape, cost, limit=SMALL, **kwargs):
    flops, moved = cost
    return pl.pallas_call(
        kernel,
        out_shape=out_shape,
        compiler_params=pltpu.CompilerParams(vmem_limit_bytes=limit),
        cost_estimate=pl.CostEstimate(flops=flops, bytes_accessed=moved, transcendentals=0),
        **kwargs,
    )


def bf16(*shape):
    return jax.ShapeDtypeStruct(shape, jnp.bfloat16)


def f32(*shape):
    return jax.ShapeDtypeStruct(shape, jnp.float32)


def iota(shape, dim):
    return lax.broadcasted_iota(jnp.int32, shape, dim)


def slot_matrix(group_me, across, batches, rows):
    cap = rows // 2
    count = batches * rows
    block = batches * cap
    across = across.astype(jnp.int32)
    shape = (GROUPS * block, count)
    where = iota(shape, 0)
    lane = iota(shape, 1)
    target = group_me ^ (where // block)
    routed = jnp.zeros(shape, jnp.float32)
    for k in range(across.shape[0]):
        routed = jnp.where(across[k : k + 1, :] // EXP_GRP == target, 1.0, routed)
    above, here = iota((count, count), 0), iota((count, count), 1)
    before = jnp.where((above < here) & (above // rows == here // rows), 1.0, 0.0)
    slots = jnp.dot(routed, before, preferred_element_type=jnp.float32).astype(jnp.int32)
    taken = (slots == where % cap) & (lane // rows == where % block // cap)
    return jnp.where(taken, routed, 0.0).astype(jnp.bfloat16)


def side_by_side(ref):
    batches, topk, rows = ref.shape
    shape = (rows, batches * rows)
    return sum(
        jnp.dot(
            ref[b].astype(jnp.float32),
            (iota(shape, 0) + b * rows == iota(shape, 1)).astype(jnp.float32),
            preferred_element_type=jnp.float32,
        )
        for b in range(batches)
    )


def prep_kernel(group_ref, *refs):
    given, (matrix_ref, *out_refs, tokens_ref, ids_ref, weights_ref, sem) = refs[:3], refs[3:]
    batches, rows, width = tokens_ref.shape
    copies = [
        pltpu.make_async_copy(source, ref, sem.at[n])
        for n, (source, ref) in enumerate(zip(given, (tokens_ref, ids_ref, weights_ref)))
    ]
    for copy in copies:
        copy.start()
    copies[1].wait()
    copies[2].wait()
    ids, weights = side_by_side(ids_ref), side_by_side(weights_ref)
    matrix = slot_matrix(group_ref[0], ids, batches, rows)
    matrix_ref[...] = matrix
    block = matrix.shape[0] // GROUPS
    copies[0].wait()
    tokens = tokens_ref[...].reshape(batches * rows, width)
    bucket = jnp.dot(matrix, tokens, preferred_element_type=jnp.float32)
    more = [
        lax.dot_general(
            matrix.astype(jnp.float32),
            values,
            (((1,), (1,)), ((), ())),
            preferred_element_type=jnp.float32,
        )
        for values in (ids, weights)
    ]
    pad = jnp.zeros((matrix.shape[0], EXTRA - 2 * ids.shape[0]), jnp.float32)
    more = jnp.concatenate(more + [pad], axis=1)
    for t, out in enumerate(out_refs):
        out[:, :width] = bucket[t * block : (t + 1) * block].astype(jnp.bfloat16)
        out[:, width:] = more[t * block : (t + 1) * block].astype(jnp.bfloat16)


def join_kernel(*refs):
    refs[-1][...] = jnp.concatenate(
        [r[...].astype(jnp.float32) for r in refs[:-1]], axis=0
    ).astype(jnp.bfloat16)


def fetch_kernel(after_ref, w_ref, out_ref, sem):
    del after_ref
    copies = [
        pltpu.make_async_copy(
            w_ref.at[0, d : d + DEPTH], out_ref.at[d : d + DEPTH], sem.at[d // DEPTH]
        )
        for d in range(0, out_ref.shape[0], DEPTH)
    ]
    for copy in copies:
        copy.start()
    for copy in copies:
        copy.wait()


def expert_kernel(parts, topk, expert_ref, *refs):
    xs, refs = refs[:parts], refs[parts:]
    w_gate_ref, w_rest_ref, w_up_ref, w_down_ref, kept_ref, away_ref = refs[:6]
    gate_acc, up_acc, hidden, up_slots, up_sem, down_slots, down_sem = refs[6:]
    half, width = kept_ref.shape
    ups, downs = width // DEPTH, width // COLUMNS
    held = w_gate_ref.shape[0] // DEPTH
    here = [slice(i * DEPTH, (i + 1) * DEPTH) for i in range(ups)]
    sources = []
    for i in range(ups):
        if i >= held:
            sources.append(w_rest_ref.at[0, here[i]])
        sources.append(w_up_ref.at[0, here[i]])
    count = len(sources)
    copies = [
        pltpu.make_async_copy(source, up_slots.at[n % AHEAD], up_sem.at[n % AHEAD])
        for n, source in enumerate(sources)
    ] + [
        pltpu.make_async_copy(
            w_down_ref.at[0, :, j * COLUMNS : (j + 1) * COLUMNS],
            down_slots.at[j % AHEAD],
            down_sem.at[j % AHEAD],
        )
        for j in range(downs)
    ]
    for copy in copies[:AHEAD]:
        copy.start()

    def add(acc, i, x, w):
        product = jnp.dot(x, w, preferred_element_type=jnp.float32)
        if i == 0:
            acc[...] = product
        else:
            acc[...] += product

    n = 0
    for i in range(ups):
        x = jnp.concatenate([r[:, here[i]] for r in xs], axis=0)
        if i < held:
            add(gate_acc, i, x, w_gate_ref[here[i]])
        for acc in [up_acc] if i < held else [gate_acc, up_acc]:
            copies[n].wait()
            add(acc, i, x, up_slots[n % AHEAD])
            copies[n + AHEAD].start()
            n += 1

    extra = jnp.concatenate([r[:, width:].astype(jnp.float32) for r in xs], axis=0)
    expert = expert_ref[0].astype(jnp.float32)
    column = jnp.zeros((extra.shape[0], 1), jnp.float32)
    for k in range(topk):
        column += jnp.where(
            extra[:, k : k + 1] == expert, extra[:, topk + k : topk + k + 1], 0.0
        )
    hidden[...] = (jax.nn.silu(gate_acc[...]) * up_acc[...] * column).astype(jnp.bfloat16)

    for j in range(downs):
        copies[count + j].wait()
        total = jnp.dot(hidden[...], down_slots[j % AHEAD], preferred_element_type=jnp.float32)
        at = slice(j * COLUMNS, (j + 1) * COLUMNS)
        kept_ref[:, at] = total[:half].astype(jnp.bfloat16)
        away_ref[:, at] = total[half:].astype(jnp.bfloat16)
        if j + AHEAD < downs:
            copies[count + j + AHEAD].start()


def sum_kernel(kept_ref, got_ref, *out_refs):
    total = kept_ref[...].astype(jnp.float32) + got_ref[...].astype(jnp.float32)
    block = out_refs[0].shape[0]
    for t, out in enumerate(out_refs):
        out[...] = total[t * block : (t + 1) * block].astype(jnp.bfloat16)


def mix_kernel(matrix_ref, *refs):
    out_ref = refs[-1]
    batches, rows, width = out_ref.shape
    back = jnp.concatenate([r[...].astype(jnp.float32) for r in refs[:-1]], axis=0)
    mixed = lax.dot_general(
        matrix_ref[...],
        back.astype(jnp.bfloat16),
        (((0,), (0,)), ((), ())),
        preferred_element_type=jnp.float32,
    )
    for b in range(batches):
        out_ref[b] = mixed[b * rows : (b + 1) * rows].astype(jnp.bfloat16)


def body(tokens, expert_ids, gate_weights, w_gate, w_up, w_down):
    devices = lax.axis_size("grp")
    gsize = devices // GROUPS
    in_bits = gsize.bit_length() - 1
    rank = lax.axis_index("grp")
    group_me = (rank // gsize).astype(jnp.int32)
    my_expert = (group_me * EXP_GRP + rank % gsize // (gsize // EXP_GRP)).astype(jnp.int32)
    batches, rows, width = tokens.shape
    count = batches * rows
    topk = expert_ids.shape[2]
    block = batches * (rows // 2)
    hid = w_gate.shape[2]
    total_rows = gsize * GROUPS * block
    half = total_rows // 2
    wide = width + EXTRA
    smem = pl.BlockSpec(memory_space=pltpu.SMEM)
    vmem = pl.BlockSpec(memory_space=pltpu.VMEM)
    hbm = pl.BlockSpec(memory_space=pl.ANY)

    def to_all(blocks):
        got = {by: exchanged(blocks[by], by, gsize) for by in reversed(range(1, GROUPS))}
        return [blocks[0]] + [got[by] for by in range(1, GROUPS)]

    matrix, *buckets = call(
        prep_kernel,
        [bf16(GROUPS * block, count)] + [bf16(block, wide)] * GROUPS,
        (2 * GROUPS * block * count * wide, 10 * count * wide),
        in_specs=[smem, hbm, hbm, hbm],
        out_specs=[vmem] * (1 + GROUPS),
        scratch_shapes=[
            pltpu.VMEM(tokens.shape, tokens.dtype),
            pltpu.VMEM((batches, topk, rows), expert_ids.dtype),
            pltpu.VMEM((batches, topk, rows), gate_weights.dtype),
            pltpu.SemaphoreType.DMA((3,)),
        ],
    )(
        group_me.reshape(1),
        *(
            pltpu.with_memory_space_constraint(v, pltpu.HBM)
            for v in (tokens, expert_ids.transpose(0, 2, 1), gate_weights.transpose(0, 2, 1))
        ),
    )
    w_gate, w_up, w_down = (
        pltpu.with_memory_space_constraint(w, pltpu.HBM) for w in (w_gate, w_up, w_down)
    )
    fetched = call(
        fetch_kernel,
        pltpu.VMEM((FETCHED * DEPTH, hid), jnp.bfloat16),
        (0, 4 * FETCHED * DEPTH * hid),
        in_specs=[hbm, hbm],
        out_specs=vmem,
        scratch_shapes=[pltpu.SemaphoreType.DMA((FETCHED,))],
    )(matrix, w_gate)
    fetched = pltpu.with_memory_space_constraint(fetched, pltpu.VMEM)
    parts = [
        call(
            join_kernel,
            bf16(GROUPS * block, wide),
            (0, 4 * GROUPS * block * wide),
            in_specs=[vmem] * GROUPS,
            out_specs=vmem,
        )(*to_all(buckets))
    ]
    for bit in range(in_bits):
        all_rows = parts[0] if bit == 0 else jnp.concatenate(parts)
        parts.append(exchanged(all_rows, 1 << bit, 1))

    slots = 2 * AHEAD * max(DEPTH, COLUMNS) * hid * 2
    kept, away = call(
        functools.partial(expert_kernel, len(parts), topk),
        [bf16(half, width)] * 2,
        (6 * total_rows * width * hid, 4 * width * hid),
        limit=slots + total_rows * (10 * hid + 4 * wide) + SLACK,
        in_specs=[smem] + [vmem] * (len(parts) + 1) + [hbm] * 3,
        out_specs=[vmem] * 2,
        scratch_shapes=[
            pltpu.VMEM((total_rows, hid), jnp.float32),
            pltpu.VMEM((total_rows, hid), jnp.float32),
            pltpu.VMEM((total_rows, hid), jnp.bfloat16),
            pltpu.VMEM((AHEAD, DEPTH, hid), jnp.bfloat16),
            pltpu.SemaphoreType.DMA((AHEAD,)),
            pltpu.VMEM((AHEAD, hid, COLUMNS), jnp.bfloat16),
            pltpu.SemaphoreType.DMA((AHEAD,)),
        ],
    )(my_expert.reshape(1), *parts, fetched, w_gate, w_up, w_down)

    got = exchanged(away, 1 << (in_bits - 1), 1)
    for bit in reversed(range(in_bits - 1)):
        total = kept.astype(jnp.float32) + got.astype(jnp.float32)
        quarter = total.shape[0] // 2
        kept = total[:quarter].astype(jnp.bfloat16)
        got = exchanged(total[quarter:].astype(jnp.bfloat16), 1 << bit, 1)
    results = call(
        sum_kernel,
        [bf16(block, width)] * GROUPS,
        (0, 6 * GROUPS * block * width),
        in_specs=[vmem, vmem],
        out_specs=[vmem] * GROUPS,
    )(kept, got)

    return call(
        mix_kernel,
        bf16(batches, rows, width),
        (2 * GROUPS * block * count * width, 10 * count * width),
        in_specs=[vmem] * (1 + GROUPS),
        out_specs=vmem,
    )(matrix, *to_all(results))


def solution(mesh):
    split = P(None, ("rep", "grp"), None)
    stacked = P("grp", None, None)
    return jax.shard_map(
        body,
        mesh=mesh,
        in_specs=(split, split, split, stacked, stacked, stacked),
        out_specs=split,
        check_vma=False,
    )
```

```python
import functools

import jax
import jax.numpy as jnp
from jax import lax
from jax.experimental import pallas as pl
from jax.experimental.pallas import tpu as pltpu
from jax.sharding import PartitionSpec as P

GROUPS = 8
EXP_GRP = 2
EXTRA = 128
DEPTH = 512
COLUMNS = 512
AHEAD = 4
SMALL = 8 << 20
SLACK = 1 << 20
FETCHED = 2
ORDER = (7, 6, 5, 4, 3, 2, 1)


def exchanged(shard, by, unit):
    size = lax.axis_size("grp")
    return lax.ppermute(
        shard, "grp", [(i, ((i // unit) ^ by) * unit + i % unit) for i in range(size)]
    )


def call(kernel, out_shape, cost, limit=SMALL, **kwargs):
    flops, moved = cost
    return pl.pallas_call(
        kernel,
        out_shape=out_shape,
        compiler_params=pltpu.CompilerParams(vmem_limit_bytes=limit),
        cost_estimate=pl.CostEstimate(flops=flops, bytes_accessed=moved, transcendentals=0),
        **kwargs,
    )


def bf16(*shape):
    return jax.ShapeDtypeStruct(shape, jnp.bfloat16)


def f32(*shape):
    return jax.ShapeDtypeStruct(shape, jnp.float32)


def iota(shape, dim):
    return lax.broadcasted_iota(jnp.int32, shape, dim)


def slot_matrix(group_me, across, batches, rows):
    cap = rows // 2
    count = batches * rows
    block = batches * cap
    across = across.astype(jnp.int32)
    shape = (GROUPS * block, count)
    where = iota(shape, 0)
    lane = iota(shape, 1)
    target = group_me ^ (where // block)
    routed = jnp.zeros(shape, jnp.float32)
    for k in range(across.shape[0]):
        routed = jnp.where(across[k : k + 1, :] // EXP_GRP == target, 1.0, routed)
    above, here = iota((count, count), 0), iota((count, count), 1)
    before = jnp.where((above < here) & (above // rows == here // rows), 1.0, 0.0)
    slots = jnp.dot(routed, before, preferred_element_type=jnp.float32).astype(jnp.int32)
    taken = (slots == where % cap) & (lane // rows == where % block // cap)
    return jnp.where(taken, routed, 0.0).astype(jnp.bfloat16)


def side_by_side(ref):
    batches, topk, rows = ref.shape
    shape = (rows, batches * rows)
    return sum(
        jnp.dot(
            ref[b].astype(jnp.float32),
            (iota(shape, 0) + b * rows == iota(shape, 1)).astype(jnp.float32),
            preferred_element_type=jnp.float32,
        )
        for b in range(batches)
    )


def prep_kernel(group_ref, *refs):
    given, (matrix_ref, *out_refs, tokens_ref, ids_ref, weights_ref, sem) = refs[:3], refs[3:]
    batches, rows, width = tokens_ref.shape
    copies = [
        pltpu.make_async_copy(source, ref, sem.at[n])
        for n, (source, ref) in enumerate(zip(given, (tokens_ref, ids_ref, weights_ref)))
    ]
    for copy in copies:
        copy.start()
    copies[1].wait()
    copies[2].wait()
    ids, weights = side_by_side(ids_ref), side_by_side(weights_ref)
    matrix = slot_matrix(group_ref[0], ids, batches, rows)
    matrix_ref[...] = matrix
    block = matrix.shape[0] // GROUPS
    copies[0].wait()
    tokens = tokens_ref[...].reshape(batches * rows, width)
    bucket = jnp.dot(matrix, tokens, preferred_element_type=jnp.float32)
    more = [
        lax.dot_general(
            matrix.astype(jnp.float32),
            values,
            (((1,), (1,)), ((), ())),
            preferred_element_type=jnp.float32,
        )
        for values in (ids, weights)
    ]
    pad = jnp.zeros((matrix.shape[0], EXTRA - 2 * ids.shape[0]), jnp.float32)
    more = jnp.concatenate(more + [pad], axis=1)
    for t, out in enumerate(out_refs):
        out[:, :width] = bucket[t * block : (t + 1) * block].astype(jnp.bfloat16)
        out[:, width:] = more[t * block : (t + 1) * block].astype(jnp.bfloat16)


def join_kernel(*refs):
    refs[-1][...] = jnp.concatenate(
        [r[...].astype(jnp.float32) for r in refs[:-1]], axis=0
    ).astype(jnp.bfloat16)


def fetch_kernel(after_ref, w_ref, out_ref, sem):
    del after_ref
    copies = [
        pltpu.make_async_copy(
            w_ref.at[0, d : d + DEPTH], out_ref.at[d : d + DEPTH], sem.at[d // DEPTH]
        )
        for d in range(0, out_ref.shape[0], DEPTH)
    ]
    for copy in copies:
        copy.start()
    for copy in copies:
        copy.wait()


def expert_kernel(parts, topk, expert_ref, *refs):
    xs, refs = refs[:parts], refs[parts:]
    w_gate_ref, w_rest_ref, w_up_ref, w_down_ref, kept_ref, away_ref = refs[:6]
    gate_acc, up_acc, hidden, up_slots, up_sem, down_slots, down_sem = refs[6:]
    half, width = kept_ref.shape
    ups, downs = width // DEPTH, width // COLUMNS
    held = w_gate_ref.shape[0] // DEPTH
    here = [slice(i * DEPTH, (i + 1) * DEPTH) for i in range(ups)]
    sources = []
    for i in range(ups):
        if i >= held:
            sources.append(w_rest_ref.at[0, here[i]])
        sources.append(w_up_ref.at[0, here[i]])
    count = len(sources)
    copies = [
        pltpu.make_async_copy(source, up_slots.at[n % AHEAD], up_sem.at[n % AHEAD])
        for n, source in enumerate(sources)
    ] + [
        pltpu.make_async_copy(
            w_down_ref.at[0, :, j * COLUMNS : (j + 1) * COLUMNS],
            down_slots.at[j % AHEAD],
            down_sem.at[j % AHEAD],
        )
        for j in range(downs)
    ]
    for copy in copies[:AHEAD]:
        copy.start()

    def add(acc, i, x, w):
        product = jnp.dot(x, w, preferred_element_type=jnp.float32)
        if i == 0:
            acc[...] = product
        else:
            acc[...] += product

    n = 0
    for i in range(ups):
        x = jnp.concatenate([r[:, here[i]] for r in xs], axis=0)
        if i < held:
            add(gate_acc, i, x, w_gate_ref[here[i]])
        for acc in [up_acc] if i < held else [gate_acc, up_acc]:
            copies[n].wait()
            add(acc, i, x, up_slots[n % AHEAD])
            copies[n + AHEAD].start()
            n += 1

    extra = jnp.concatenate([r[:, width:].astype(jnp.float32) for r in xs], axis=0)
    expert = expert_ref[0].astype(jnp.float32)
    column = jnp.zeros((extra.shape[0], 1), jnp.float32)
    for k in range(topk):
        column += jnp.where(
            extra[:, k : k + 1] == expert, extra[:, topk + k : topk + k + 1], 0.0
        )
    hidden[...] = (jax.nn.silu(gate_acc[...]) * up_acc[...] * column).astype(jnp.bfloat16)

    for j in range(downs):
        copies[count + j].wait()
        total = jnp.dot(hidden[...], down_slots[j % AHEAD], preferred_element_type=jnp.float32)
        at = slice(j * COLUMNS, (j + 1) * COLUMNS)
        kept_ref[:, at] = total[:half].astype(jnp.bfloat16)
        away_ref[:, at] = total[half:].astype(jnp.bfloat16)
        if j + AHEAD < downs:
            copies[count + j + AHEAD].start()


def sum_kernel(kept_ref, got_ref, *out_refs):
    total = kept_ref[...].astype(jnp.float32) + got_ref[...].astype(jnp.float32)
    block = out_refs[0].shape[0]
    for t, out in enumerate(out_refs):
        out[...] = total[t * block : (t + 1) * block].astype(jnp.bfloat16)


def mix_kernel(matrix_ref, *refs):
    out_ref = refs[-1]
    batches, rows, width = out_ref.shape
    back = jnp.concatenate([r[...].astype(jnp.float32) for r in refs[:-1]], axis=0)
    mixed = lax.dot_general(
        matrix_ref[...],
        back.astype(jnp.bfloat16),
        (((0,), (0,)), ((), ())),
        preferred_element_type=jnp.float32,
    )
    for b in range(batches):
        out_ref[b] = mixed[b * rows : (b + 1) * rows].astype(jnp.bfloat16)


def body(tokens, expert_ids, gate_weights, w_gate, w_up, w_down):
    devices = lax.axis_size("grp")
    gsize = devices // GROUPS
    in_bits = gsize.bit_length() - 1
    rank = lax.axis_index("grp")
    group_me = (rank // gsize).astype(jnp.int32)
    my_expert = (group_me * EXP_GRP + rank % gsize // (gsize // EXP_GRP)).astype(jnp.int32)
    batches, rows, width = tokens.shape
    count = batches * rows
    topk = expert_ids.shape[2]
    block = batches * (rows // 2)
    hid = w_gate.shape[2]
    total_rows = gsize * GROUPS * block
    half = total_rows // 2
    wide = width + EXTRA
    smem = pl.BlockSpec(memory_space=pltpu.SMEM)
    vmem = pl.BlockSpec(memory_space=pltpu.VMEM)
    hbm = pl.BlockSpec(memory_space=pl.ANY)

    def to_all(blocks):
        got = {by: exchanged(blocks[by], by, gsize) for by in ORDER}
        return [blocks[0]] + [got[by] for by in range(1, GROUPS)]

    matrix, *buckets = call(
        prep_kernel,
        [bf16(GROUPS * block, count)] + [bf16(block, wide)] * GROUPS,
        (2 * GROUPS * block * count * wide, 10 * count * wide),
        in_specs=[smem, hbm, hbm, hbm],
        out_specs=[vmem] * (1 + GROUPS),
        scratch_shapes=[
            pltpu.VMEM(tokens.shape, tokens.dtype),
            pltpu.VMEM((batches, topk, rows), expert_ids.dtype),
            pltpu.VMEM((batches, topk, rows), gate_weights.dtype),
            pltpu.SemaphoreType.DMA((3,)),
        ],
    )(
        group_me.reshape(1),
        *(
            pltpu.with_memory_space_constraint(v, pltpu.HBM)
            for v in (tokens, expert_ids.transpose(0, 2, 1), gate_weights.transpose(0, 2, 1))
        ),
    )
    w_gate, w_up, w_down = (
        pltpu.with_memory_space_constraint(w, pltpu.HBM) for w in (w_gate, w_up, w_down)
    )
    fetched = call(
        fetch_kernel,
        pltpu.VMEM((FETCHED * DEPTH, hid), jnp.bfloat16),
        (0, 4 * FETCHED * DEPTH * hid),
        in_specs=[hbm, hbm],
        out_specs=vmem,
        scratch_shapes=[pltpu.SemaphoreType.DMA((FETCHED,))],
    )(matrix, w_gate)
    fetched = pltpu.with_memory_space_constraint(fetched, pltpu.VMEM)
    blocks = to_all(buckets)
    near, far = blocks[: GROUPS // 2], blocks[GROUPS // 2 :]
    parts = []
    for side in (near, far):
        if parts:
            side, parts = lax.optimization_barrier((side, parts))
        parts = parts + [
            call(
                join_kernel,
                bf16(GROUPS // 2 * block, wide),
                (0, 2 * GROUPS * block * wide),
                in_specs=[vmem] * (GROUPS // 2),
                out_specs=vmem,
            )(*side)
        ]
    for bit in range(in_bits):
        parts += [exchanged(part, 1 << bit, 1) for part in parts]

    slots = 2 * AHEAD * max(DEPTH, COLUMNS) * hid * 2
    kept, away = call(
        functools.partial(expert_kernel, len(parts), topk),
        [bf16(half, width)] * 2,
        (6 * total_rows * width * hid, 4 * width * hid),
        limit=slots + total_rows * (10 * hid + 4 * wide) + SLACK,
        in_specs=[smem] + [vmem] * (len(parts) + 1) + [hbm] * 3,
        out_specs=[vmem] * 2,
        scratch_shapes=[
            pltpu.VMEM((total_rows, hid), jnp.float32),
            pltpu.VMEM((total_rows, hid), jnp.float32),
            pltpu.VMEM((total_rows, hid), jnp.bfloat16),
            pltpu.VMEM((AHEAD, DEPTH, hid), jnp.bfloat16),
            pltpu.SemaphoreType.DMA((AHEAD,)),
            pltpu.VMEM((AHEAD, hid, COLUMNS), jnp.bfloat16),
            pltpu.SemaphoreType.DMA((AHEAD,)),
        ],
    )(my_expert.reshape(1), *parts, fetched, w_gate, w_up, w_down)

    got = exchanged(away, 1 << (in_bits - 1), 1)
    for bit in reversed(range(in_bits - 1)):
        total = kept.astype(jnp.float32) + got.astype(jnp.float32)
        quarter = total.shape[0] // 2
        kept = total[:quarter].astype(jnp.bfloat16)
        got = exchanged(total[quarter:].astype(jnp.bfloat16), 1 << bit, 1)
    results = call(
        sum_kernel,
        [bf16(block, width)] * GROUPS,
        (0, 6 * GROUPS * block * width),
        in_specs=[vmem, vmem],
        out_specs=[vmem] * GROUPS,
    )(kept, got)

    return call(
        mix_kernel,
        bf16(batches, rows, width),
        (2 * GROUPS * block * count * width, 10 * count * width),
        in_specs=[vmem] * (1 + GROUPS),
        out_specs=vmem,
    )(matrix, *to_all(results))


def solution(mesh):
    split = P(None, ("rep", "grp"), None)
    stacked = P("grp", None, None)
    return jax.shard_map(
        body,
        mesh=mesh,
        in_specs=(split, split, split, stacked, stacked, stacked),
        out_specs=split,
        check_vma=False,
    )
```

```python
import functools

import jax
import jax.numpy as jnp
from jax import lax
from jax.experimental import pallas as pl
from jax.experimental.pallas import tpu as pltpu
from jax.sharding import PartitionSpec as P

GROUPS = 8
EXP_GRP = 2
EXTRA = 128
DEPTH = 512
COLUMNS = 512
AHEAD = 4
SMALL = 8 << 20
SLACK = 1 << 20
FETCHED = 1
ORDER = (7, 6, 5, 4, 3, 2, 1)


def exchanged(shard, by, unit):
    size = lax.axis_size("grp")
    return lax.ppermute(
        shard, "grp", [(i, ((i // unit) ^ by) * unit + i % unit) for i in range(size)]
    )


def call(kernel, out_shape, cost, limit=SMALL, **kwargs):
    flops, moved = cost
    return pl.pallas_call(
        kernel,
        out_shape=out_shape,
        compiler_params=pltpu.CompilerParams(vmem_limit_bytes=limit),
        cost_estimate=pl.CostEstimate(flops=flops, bytes_accessed=moved, transcendentals=0),
        **kwargs,
    )


def bf16(*shape):
    return jax.ShapeDtypeStruct(shape, jnp.bfloat16)


def f32(*shape):
    return jax.ShapeDtypeStruct(shape, jnp.float32)


def iota(shape, dim):
    return lax.broadcasted_iota(jnp.int32, shape, dim)


def slot_matrix(group_me, across, batches, rows):
    cap = rows // 2
    count = batches * rows
    block = batches * cap
    across = across.astype(jnp.int32)
    shape = (GROUPS * block, count)
    where = iota(shape, 0)
    lane = iota(shape, 1)
    target = group_me ^ (where // block)
    routed = jnp.zeros(shape, jnp.float32)
    for k in range(across.shape[0]):
        routed = jnp.where(across[k : k + 1, :] // EXP_GRP == target, 1.0, routed)
    above, here = iota((count, count), 0), iota((count, count), 1)
    before = jnp.where((above < here) & (above // rows == here // rows), 1.0, 0.0)
    slots = jnp.dot(routed, before, preferred_element_type=jnp.float32).astype(jnp.int32)
    taken = (slots == where % cap) & (lane // rows == where % block // cap)
    return jnp.where(taken, routed, 0.0).astype(jnp.bfloat16)


def side_by_side(ref):
    batches, topk, rows = ref.shape
    shape = (rows, batches * rows)
    return sum(
        jnp.dot(
            ref[b].astype(jnp.float32),
            (iota(shape, 0) + b * rows == iota(shape, 1)).astype(jnp.float32),
            preferred_element_type=jnp.float32,
        )
        for b in range(batches)
    )


def prep_kernel(group_ref, *refs):
    given, (matrix_ref, *out_refs, tokens_ref, ids_ref, weights_ref, sem) = refs[:3], refs[3:]
    batches, rows, width = tokens_ref.shape
    copies = [
        pltpu.make_async_copy(source, ref, sem.at[n])
        for n, (source, ref) in enumerate(zip(given, (tokens_ref, ids_ref, weights_ref)))
    ]
    for copy in copies:
        copy.start()
    copies[1].wait()
    copies[2].wait()
    ids, weights = side_by_side(ids_ref), side_by_side(weights_ref)
    matrix = slot_matrix(group_ref[0], ids, batches, rows)
    matrix_ref[...] = matrix
    block = matrix.shape[0] // GROUPS
    copies[0].wait()
    tokens = tokens_ref[...].reshape(batches * rows, width)
    bucket = jnp.dot(matrix, tokens, preferred_element_type=jnp.float32)
    more = [
        lax.dot_general(
            matrix.astype(jnp.float32),
            values,
            (((1,), (1,)), ((), ())),
            preferred_element_type=jnp.float32,
        )
        for values in (ids, weights)
    ]
    pad = jnp.zeros((matrix.shape[0], EXTRA - 2 * ids.shape[0]), jnp.float32)
    more = jnp.concatenate(more + [pad], axis=1)
    for t, out in enumerate(out_refs):
        out[:, :width] = bucket[t * block : (t + 1) * block].astype(jnp.bfloat16)
        out[:, width:] = more[t * block : (t + 1) * block].astype(jnp.bfloat16)


def join_kernel(*refs):
    refs[-1][...] = jnp.concatenate(
        [r[...].astype(jnp.float32) for r in refs[:-1]], axis=0
    ).astype(jnp.bfloat16)


def fetch_kernel(after_ref, w_ref, out_ref, sem):
    del after_ref
    copies = [
        pltpu.make_async_copy(
            w_ref.at[0, d : d + DEPTH], out_ref.at[d : d + DEPTH], sem.at[d // DEPTH]
        )
        for d in range(0, out_ref.shape[0], DEPTH)
    ]
    for copy in copies:
        copy.start()
    for copy in copies:
        copy.wait()


def expert_kernel(parts, topk, expert_ref, *refs):
    xs, refs = refs[:parts], refs[parts:]
    w_gate_ref, w_rest_ref, w_up_ref, w_down_ref, kept_ref, away_ref = refs[:6]
    gate_acc, up_acc, hidden, up_slots, up_sem, down_slots, down_sem = refs[6:]
    half, width = kept_ref.shape
    ups, downs = width // DEPTH, width // COLUMNS
    held = w_gate_ref.shape[0] // DEPTH
    here = [slice(i * DEPTH, (i + 1) * DEPTH) for i in range(ups)]
    sources = []
    for i in range(ups):
        if i >= held:
            sources.append(w_rest_ref.at[0, here[i]])
        sources.append(w_up_ref.at[0, here[i]])
    count = len(sources)
    copies = [
        pltpu.make_async_copy(source, up_slots.at[n % AHEAD], up_sem.at[n % AHEAD])
        for n, source in enumerate(sources)
    ] + [
        pltpu.make_async_copy(
            w_down_ref.at[0, :, j * COLUMNS : (j + 1) * COLUMNS],
            down_slots.at[j % AHEAD],
            down_sem.at[j % AHEAD],
        )
        for j in range(downs)
    ]
    for copy in copies[:AHEAD]:
        copy.start()

    def add(acc, i, x, w):
        product = jnp.dot(x, w, preferred_element_type=jnp.float32)
        if i == 0:
            acc[...] = product
        else:
            acc[...] += product

    n = 0
    for i in range(ups):
        x = jnp.concatenate([r[:, here[i]] for r in xs], axis=0)
        if i < held:
            add(gate_acc, i, x, w_gate_ref[here[i]])
        for acc in [up_acc] if i < held else [gate_acc, up_acc]:
            copies[n].wait()
            add(acc, i, x, up_slots[n % AHEAD])
            copies[n + AHEAD].start()
            n += 1

    extra = jnp.concatenate([r[:, width:].astype(jnp.float32) for r in xs], axis=0)
    expert = expert_ref[0].astype(jnp.float32)
    column = jnp.zeros((extra.shape[0], 1), jnp.float32)
    for k in range(topk):
        column += jnp.where(
            extra[:, k : k + 1] == expert, extra[:, topk + k : topk + k + 1], 0.0
        )
    hidden[...] = (jax.nn.silu(gate_acc[...]) * up_acc[...] * column).astype(jnp.bfloat16)

    for j in range(downs):
        copies[count + j].wait()
        total = jnp.dot(hidden[...], down_slots[j % AHEAD], preferred_element_type=jnp.float32)
        at = slice(j * COLUMNS, (j + 1) * COLUMNS)
        kept_ref[:, at] = total[:half].astype(jnp.bfloat16)
        away_ref[:, at] = total[half:].astype(jnp.bfloat16)
        if j + AHEAD < downs:
            copies[count + j + AHEAD].start()


def sum_kernel(kept_ref, got_ref, *out_refs):
    total = kept_ref[...].astype(jnp.float32) + got_ref[...].astype(jnp.float32)
    block = out_refs[0].shape[0]
    for t, out in enumerate(out_refs):
        out[...] = total[t * block : (t + 1) * block].astype(jnp.bfloat16)


def mix_kernel(matrix_ref, *refs):
    out_ref = refs[-1]
    batches, rows, width = out_ref.shape
    back = jnp.concatenate([r[...].astype(jnp.float32) for r in refs[:-1]], axis=0)
    mixed = lax.dot_general(
        matrix_ref[...],
        back.astype(jnp.bfloat16),
        (((0,), (0,)), ((), ())),
        preferred_element_type=jnp.float32,
    )
    for b in range(batches):
        out_ref[b] = mixed[b * rows : (b + 1) * rows].astype(jnp.bfloat16)


def body(tokens, expert_ids, gate_weights, w_gate, w_up, w_down):
    devices = lax.axis_size("grp")
    gsize = devices // GROUPS
    in_bits = gsize.bit_length() - 1
    rank = lax.axis_index("grp")
    group_me = (rank // gsize).astype(jnp.int32)
    my_expert = (group_me * EXP_GRP + rank % gsize // (gsize // EXP_GRP)).astype(jnp.int32)
    batches, rows, width = tokens.shape
    count = batches * rows
    topk = expert_ids.shape[2]
    block = batches * (rows // 2)
    hid = w_gate.shape[2]
    total_rows = gsize * GROUPS * block
    half = total_rows // 2
    wide = width + EXTRA
    smem = pl.BlockSpec(memory_space=pltpu.SMEM)
    vmem = pl.BlockSpec(memory_space=pltpu.VMEM)
    hbm = pl.BlockSpec(memory_space=pl.ANY)

    def to_all(blocks):
        got = {by: exchanged(blocks[by], by, gsize) for by in ORDER}
        return [blocks[0]] + [got[by] for by in range(1, GROUPS)]

    matrix, *buckets = call(
        prep_kernel,
        [bf16(GROUPS * block, count)] + [bf16(block, wide)] * GROUPS,
        (2 * GROUPS * block * count * wide, 10 * count * wide),
        in_specs=[smem, hbm, hbm, hbm],
        out_specs=[vmem] * (1 + GROUPS),
        scratch_shapes=[
            pltpu.VMEM(tokens.shape, tokens.dtype),
            pltpu.VMEM((batches, topk, rows), expert_ids.dtype),
            pltpu.VMEM((batches, topk, rows), gate_weights.dtype),
            pltpu.SemaphoreType.DMA((3,)),
        ],
    )(
        group_me.reshape(1),
        *(
            pltpu.with_memory_space_constraint(v, pltpu.HBM)
            for v in (tokens, expert_ids.transpose(0, 2, 1), gate_weights.transpose(0, 2, 1))
        ),
    )
    w_gate, w_up, w_down = (
        pltpu.with_memory_space_constraint(w, pltpu.HBM) for w in (w_gate, w_up, w_down)
    )
    fetched = call(
        fetch_kernel,
        pltpu.VMEM((FETCHED * DEPTH, hid), jnp.bfloat16),
        (0, 4 * FETCHED * DEPTH * hid),
        in_specs=[hbm, hbm],
        out_specs=vmem,
        scratch_shapes=[pltpu.SemaphoreType.DMA((FETCHED,))],
    )(matrix, w_gate)
    fetched = pltpu.with_memory_space_constraint(fetched, pltpu.VMEM)
    blocks = to_all(buckets)
    near, far = blocks[: GROUPS // 2], blocks[GROUPS // 2 :]
    parts = []
    for side in (near, far):
        if parts:
            side, parts = lax.optimization_barrier((side, parts))
        parts = parts + [
            call(
                join_kernel,
                bf16(GROUPS // 2 * block, wide),
                (0, 2 * GROUPS * block * wide),
                in_specs=[vmem] * (GROUPS // 2),
                out_specs=vmem,
            )(*side)
        ]
    for bit in range(in_bits):
        parts += [exchanged(part, 1 << bit, 1) for part in parts]

    slots = 2 * AHEAD * max(DEPTH, COLUMNS) * hid * 2
    kept, away = call(
        functools.partial(expert_kernel, len(parts), topk),
        [bf16(half, width)] * 2,
        (6 * total_rows * width * hid, 4 * width * hid),
        limit=slots + total_rows * (10 * hid + 4 * wide) + SLACK,
        in_specs=[smem] + [vmem] * (len(parts) + 1) + [hbm] * 3,
        out_specs=[vmem] * 2,
        scratch_shapes=[
            pltpu.VMEM((total_rows, hid), jnp.float32),
            pltpu.VMEM((total_rows, hid), jnp.float32),
            pltpu.VMEM((total_rows, hid), jnp.bfloat16),
            pltpu.VMEM((AHEAD, DEPTH, hid), jnp.bfloat16),
            pltpu.SemaphoreType.DMA((AHEAD,)),
            pltpu.VMEM((AHEAD, hid, COLUMNS), jnp.bfloat16),
            pltpu.SemaphoreType.DMA((AHEAD,)),
        ],
    )(my_expert.reshape(1), *parts, fetched, w_gate, w_up, w_down)

    got = exchanged(away, 1 << (in_bits - 1), 1)
    for bit in reversed(range(in_bits - 1)):
        total = kept.astype(jnp.float32) + got.astype(jnp.float32)
        quarter = total.shape[0] // 2
        kept = total[:quarter].astype(jnp.bfloat16)
        got = exchanged(total[quarter:].astype(jnp.bfloat16), 1 << bit, 1)
    results = call(
        sum_kernel,
        [bf16(block, width)] * GROUPS,
        (0, 6 * GROUPS * block * width),
        in_specs=[vmem, vmem],
        out_specs=[vmem] * GROUPS,
    )(kept, got)

    return call(
        mix_kernel,
        bf16(batches, rows, width),
        (2 * GROUPS * block * count * width, 10 * count * width),
        in_specs=[vmem] * (1 + GROUPS),
        out_specs=vmem,
    )(matrix, *to_all(results))


def solution(mesh):
    split = P(None, ("rep", "grp"), None)
    stacked = P("grp", None, None)
    return jax.shard_map(
        body,
        mesh=mesh,
        in_specs=(split, split, split, stacked, stacked, stacked),
        out_specs=split,
        check_vma=False,
    )
```
